128 devices in a mesh: dp: 16 (over x, y), tensor: 8 (over z, core).
Axes of the slice: x: 4, y: 4, z: 4, core: 2. Of those that a mesh axis runs over, the one named last changes fastest.
Arguments:
- activations: bfloat16 [4096, 5120], P('dp'), may hold values from -6 to 6
- out_grad: bfloat16 [4096, 5120], P('dp'), may hold values from -85 to 85, as said below
- gate_pre: bfloat16 [4096, 13824], P('dp', 'tensor'), may hold values from -6 to 6
- up_pre: bfloat16 [4096, 13824], P('dp', 'tensor'), may hold values from -26 to 26
- down_weight: bfloat16 [5120, 13824], P(None, 'tensor'), may hold values from -0.0546875 to 0.0546875
- clip_bounds: float32 [2], replicated, may hold values from 1.5 to 4
Outputs:
- grad_down: bfloat16 [5120, 13824], P('dp', 'tensor')
- grad_gate: bfloat16 [5120, 13824], P('dp', 'tensor')
The draws below stay inside these ranges and needn't reach their ends.
Inputs may be any that keep to these rules, and one draw needn't show every extreme that they name: out_grad has a common scale within each example.
All inputs are finite; a program needn't handle non-finite values.
Results may differ from the reference program's by a relative error of at most 0.019.
Values may be sent and summed in bfloat16 or wider, within the bound.
No kernel may reach another device: no remote copies, remote signals or barrier semaphores. Data moves between devices by JAX's collectives and lax.ppermute only.
A program may use at most 192 MiB of HBM per device.

```python
import math
import jax
import jax.numpy as jnp
from jax import lax

D = 5120
FF = 13824
SEQ = 256
TOK_DEV = 256
TOKENS = 4096
EXAMPLES = 16


def draw_out_grad(key, part):
    key = jax.random.fold_in(key, 11)
    key_base, key_jitter = jax.random.split(key, 2)
    example_total = TOKENS // SEQ
    ramp = 10.0 ** (jnp.arange(example_total, dtype=jnp.float32) / max(example_total - 1, 1))
    jitter = jnp.exp(jax.random.uniform(key_jitter, (example_total,), jnp.float32, math.log(0.7), math.log(1.4)))
    base = jnp.clip(jax.random.normal(key_base, (TOKENS, D), jnp.float32), -6.0, 6.0)
    row_scale = jnp.repeat(ramp * jitter, SEQ)[:, None]
    return (base * row_scale).astype(jnp.bfloat16)


def draw_up_pre(key, part):
    key = jax.random.fold_in(key, 23)
    key_base, key_jitter = jax.random.split(key, 2)
    position = jnp.arange(FF, dtype=jnp.float32) / max(FF - 1, 1)
    jitter = jnp.exp(jax.random.uniform(key_jitter, (FF,), jnp.float32, math.log(0.7), math.log(1.4)))
    base = jnp.clip(jax.random.normal(key_base, (TOKENS, FF), jnp.float32), -6.0, 6.0)
    column_scale = 3.0 ** position * jitter
    return (base * column_scale[None, :]).astype(jnp.bfloat16)


def levels(rng, dims, shards, low, largest):
    def one(axis_at, parts):
        steps = jax.random.uniform(jax.random.fold_in(jax.random.fold_in(rng, 6), axis_at), (parts,), jnp.float32, low / len(shards), largest / len(shards))
        return jnp.repeat(jnp.exp(steps), dims[axis_at] // parts).reshape((-1,) + (1,) * (len(dims) - axis_at - 1))

    level = one(*shards[0])
    for cut in shards[1:]:
        level = level * one(*cut)
    return level


def gaussian(stream_key, dims, deviation, bound, cuts=(), held_as=jnp.bfloat16):
    values = deviation * jax.random.normal(stream_key, dims, jnp.float32)
    if cuts:
        values = values * levels(stream_key, dims, cuts, -0.22, 0.18)
    return jnp.clip(values, -bound, bound).astype(held_as)


def setup_inputs(seed: int = 0) -> dict:
    key_of = jax.random.split(jax.random.key(seed), 7)
    return {
        "activations": gaussian(key_of[0], (TOKENS, D), 1.0, 6.0, ((0, 16),)),
        "out_grad": draw_out_grad(jax.random.fold_in(key_of[6], 71), 0),
        "gate_pre": gaussian(key_of[2], (TOKENS, FF), 1.0, 6.0, ((0, 16), (1, 8))),
        "up_pre": draw_up_pre(jax.random.fold_in(key_of[6], 71), 0),
        "down_weight": gaussian(key_of[4], (D, FF), FF ** -0.5, 0.0546875, ((1, 8),)),
        "clip_bounds": jnp.clip(jnp.exp(jax.random.uniform(key_of[5], (2,), jnp.float32, math.log(1.5), math.log(4.0))), 1.5, 4.0),
    }


def silu_slope(values):
    sigma = jax.nn.sigmoid(values)
    return sigma * (1.0 + values * (1.0 - sigma))

def pair_gram(matrix):
    return lax.dot_general(matrix, matrix, (((1,), (1,)), ((), ())), preferred_element_type=jnp.float32)

def reference(activations, out_grad, gate_pre, up_pre, down_weight, clip_bounds):
    gate_val = gate_pre.astype(jnp.float32)
    up_val = up_pre.astype(jnp.float32)
    hidden = (jax.nn.silu(gate_val) * up_val).astype(jnp.bfloat16)
    hidden_grad = jnp.dot(out_grad, down_weight, preferred_element_type=jnp.float32)
    gate_grad = (hidden_grad * up_val * silu_slope(gate_val)).astype(jnp.bfloat16)

    def example_squares(example):
        begin_row = (example * SEQ).astype(jnp.int32)
        x_rows = lax.dynamic_slice_in_dim(activations, begin_row, SEQ, 0)
        o_rows = lax.dynamic_slice_in_dim(out_grad, begin_row, SEQ, 0)
        h_rows = lax.dynamic_slice_in_dim(hidden, begin_row, SEQ, 0)
        g_rows = lax.dynamic_slice_in_dim(gate_grad, begin_row, SEQ, 0)
        down_sq = jnp.sum(pair_gram(h_rows) * pair_gram(o_rows))
        gate_sq = jnp.sum(pair_gram(x_rows) * pair_gram(g_rows))
        return jnp.stack([down_sq, gate_sq])
    squares = lax.map(example_squares, jnp.arange(EXAMPLES, dtype=jnp.int32))
    radius = clip_bounds.astype(jnp.float32) * math.sqrt(float(D * FF * SEQ))
    factor = radius / jnp.maximum(jnp.sqrt(squares), radius)
    row_factor = jnp.repeat(factor, SEQ, axis=0)
    scaled_hidden = (row_factor[:, 0:1] * hidden.astype(jnp.float32)).astype(jnp.bfloat16)
    scaled_gate_grad = (row_factor[:, 1:2] * gate_grad.astype(jnp.float32)).astype(jnp.bfloat16)

    def add_block(totals, block):
        begin_row = (block * TOK_DEV).astype(jnp.int32)
        x_rows = lax.dynamic_slice_in_dim(activations, begin_row, TOK_DEV, 0)
        o_rows = lax.dynamic_slice_in_dim(out_grad, begin_row, TOK_DEV, 0)
        h_rows = lax.dynamic_slice_in_dim(scaled_hidden, begin_row, TOK_DEV, 0)
        g_rows = lax.dynamic_slice_in_dim(scaled_gate_grad, begin_row, TOK_DEV, 0)
        down_part = lax.dot_general(o_rows, h_rows, (((0,), (0,)), ((), ())), preferred_element_type=jnp.float32)
        gate_part = lax.dot_general(x_rows, g_rows, (((0,), (0,)), ((), ())), preferred_element_type=jnp.float32)
        down_part = lax.optimization_barrier(down_part.astype(jnp.bfloat16)).astype(jnp.float32)
        gate_part = lax.optimization_barrier(gate_part.astype(jnp.bfloat16)).astype(jnp.float32)
        return ((totals[0] + down_part, totals[1] + gate_part), None)
    start_sums = (jnp.zeros((D, FF), jnp.float32), jnp.zeros((D, FF), jnp.float32))
    sums, _ = lax.scan(add_block, start_sums, jnp.arange(TOKENS // TOK_DEV, dtype=jnp.int32))
    grad_down = (sums[0] / EXAMPLES).astype(jnp.bfloat16)
    grad_gate = (sums[1] / EXAMPLES).astype(jnp.bfloat16)
    return (grad_down, grad_gate)
```

```python
import math

import jax
import jax.numpy as jnp
from jax import lax
from jax.sharding import Mesh, PartitionSpec as P

SEQ = 256
RING = 4


def silu_slope(values):
    sigma = jax.nn.sigmoid(values)
    return sigma * (1.0 + values * (1.0 - sigma))


def shift(value, axis, step):
    return lax.ppermute(value, axis, [(i, (i + step) % RING) for i in range(RING)])


def swap_cores(value):
    return lax.ppermute(value, "core", [(0, 1), (1, 0)])


def ring_gather(value, axis):
    half = value.shape[0] // 2
    before = shift(value, axis, 1)
    after = shift(value, axis, -1)
    far_top = shift(before[:half], axis, 1)
    far_bottom = shift(after[half:], axis, -1)
    return [value, before, after, jnp.concatenate([far_top, far_bottom], axis=0)]


def ring_reduce(piece, axis):
    far = piece(2).astype(jnp.bfloat16)
    half = far.shape[0] // 2
    far_up = shift(far[:half], axis, 1)
    far_down = shift(far[half:], axis, -1)
    after = piece(1)
    before = piece(-1)
    near_up = shift(after[half:].astype(jnp.bfloat16), axis, 1)
    near_down = shift(before[:half].astype(jnp.bfloat16), axis, -1)
    own = piece(0)
    sum_up = shift((after[:half] + far_up.astype(jnp.float32)).astype(jnp.bfloat16), axis, 1)
    sum_down = shift((before[half:] + far_down.astype(jnp.float32)).astype(jnp.bfloat16), axis, -1)
    top = own[:half] + near_down.astype(jnp.float32) + sum_up.astype(jnp.float32)
    bottom = own[half:] + near_up.astype(jnp.float32) + sum_down.astype(jnp.float32)
    return jnp.concatenate([top, bottom], axis=0)


def dot_last(left, right):
    return lax.dot_general(left, right, (((1,), (1,)), ((), ())), preferred_element_type=jnp.float32)


def dot_first(left, right):
    return lax.dot_general(left, right, (((0,), (0,)), ((), ())), preferred_element_type=jnp.float32)


def spread_columns(turned, row_start, axis):
    place = lax.axis_index(axis)
    rows = turned.shape[0] // 32

    def part(step):
        return lax.dynamic_slice_in_dim(turned, row_start((place + step) % RING), rows, 0)

    own = part(0)
    blocks = [own, shift(part(1), axis, 1), shift(part(-1), axis, -1), shift(part(2), axis, 2)]
    share = jnp.concatenate(blocks, axis=1)
    own_z, before, after, far = ring_gather(share, "z")
    mine = jnp.stack([own_z, after, far, before])
    other = swap_cores(mine)
    is_first = lax.axis_index("core") == 0
    low = jnp.where(is_first, mine, other)
    high = jnp.where(is_first, other, mine)
    return jnp.concatenate([low, high], axis=1)


def local(activations, out_grad, gate_pre, up_pre, down_weight, clip_bounds):
    model_width = activations.shape[1]
    full_hidden = gate_pre.shape[1] * lax.axis_size("z") * lax.axis_size("core")
    example_total = lax.axis_size("x") * lax.axis_size("y")
    at_x, at_y, at_z, at_core = (lax.axis_index(a) for a in ("x", "y", "z", "core"))
    owned = model_width // example_total

    gate_val = gate_pre.T.astype(jnp.float32)
    up_val = up_pre.T.astype(jnp.float32)
    hidden = (jax.nn.silu(gate_val) * up_val).astype(jnp.bfloat16)
    hidden_blocks = ring_gather(hidden, "x")

    half = at_core * (owned // 2)
    out_cols = spread_columns(out_grad.T, lambda x: x * (4 * owned) + at_z * owned + half, "x")
    act_cols = spread_columns(activations.T, lambda y: at_z * (4 * owned) + y * owned + half, "y")

    hidden_grad = dot_last(down_weight.T, out_grad)
    gate_grad = (hidden_grad * up_val * silu_slope(gate_val)).astype(jnp.bfloat16)
    gate_blocks = ring_gather(gate_grad, "y")

    down_sq = jnp.sum(dot_first(hidden, hidden) * dot_last(out_grad, out_grad))
    gate_sq = jnp.sum(dot_last(activations, activations) * dot_first(gate_grad, gate_grad))
    squares = jnp.stack([down_sq, gate_sq])[:, None] * jnp.ones((2, 128), jnp.float32)
    squares = squares + swap_cores(squares)
    squares = squares + shift(squares, "z", 1) + shift(squares, "z", -1) + shift(squares, "z", 2)
    radius = (clip_bounds * math.sqrt(float(model_width * full_hidden * SEQ)))[:, None]
    factor = radius / jnp.maximum(jnp.sqrt(squares), radius)
    down_factors = [factor] + [shift(factor, "x", s) for s in (1, -1, 2)]
    gate_factors = [factor] + [shift(factor, "y", s) for s in (1, -1, 2)]

    def scaled(blocks, factors, layer):
        return jnp.concatenate(
            [
                (f[layer, 0] * b.astype(jnp.float32)).astype(jnp.bfloat16)
                for b, f in zip(blocks, factors, strict=True)
            ],
            axis=1,
        )

    scaled_hidden = scaled(hidden_blocks, down_factors, 0)
    scaled_gate = scaled(gate_blocks, gate_factors, 1)

    def down_piece(step):
        cols = lax.dynamic_index_in_dim(out_cols, (at_y + step - at_z) % RING, 0, keepdims=False)
        return dot_last(cols, scaled_hidden)

    def gate_piece(step):
        cols = lax.dynamic_index_in_dim(act_cols, (at_x + step - at_z) % RING, 0, keepdims=False)
        return dot_last(cols, scaled_gate)

    grad_down = (ring_reduce(down_piece, "y") / example_total).astype(jnp.bfloat16)
    grad_gate = (ring_reduce(gate_piece, "x") / example_total).astype(jnp.bfloat16)
    return (grad_down, grad_gate)


def solution(mesh):
    torus = Mesh(mesh.devices.reshape(RING, RING, RING, 2), ("x", "y", "z", "core"))
    dp, tensor = ("x", "y"), ("z", "core")
    in_specs = (P(dp, None), P(dp, None), P(dp, tensor), P(dp, tensor), P(None, tensor), P())
    out_specs = (P(dp, tensor), P(dp, tensor))
    return jax.shard_map(local, mesh=torus, in_specs=in_specs, out_specs=out_specs, check_vma=False)
```

```python
import functools
import math

import jax
import jax.numpy as jnp
from jax import lax
from jax.experimental import pallas as pl
from jax.experimental.pallas import tpu as pltpu
from jax.sharding import Mesh, PartitionSpec as P

SEQ = 256
RING = 4
CORES = 2
STEPS = (0, 1, -1, 2)
LANES = 128
MIB = 1024 * 1024
HEAVY = pl.CostEstimate(flops=10**12, bytes_accessed=10**9, transcendentals=0)
SMALL = pl.CostEstimate(flops=0, bytes_accessed=0, transcendentals=0)


def move(value, axes, goal):
    pairs = []
    for x in range(RING):
        for y in range(RING):
            for core in range(2):
                to_x, to_y = goal(x, y, core)
                pairs.append(((x * RING + y) * 2 + core, (to_x % RING * RING + to_y % RING) * 2 + core))
    return lax.ppermute(value, axes, pairs)


def shift(value, axis, step):
    if axis != "spread":
        return lax.ppermute(value, axis, [(i, (i + step) % RING) for i in range(RING)])
    pairs = []
    for x in range(RING):
        for y in range(RING):
            for core in range(2):
                to_x, to_y = ((x + step) % RING, y) if core == 0 else (x, (y + step) % RING)
                pairs.append(((x * RING + y) * 2 + core, (to_x * RING + to_y) * 2 + core))
    return lax.ppermute(value, ("x", "y", "core"), pairs)


def swap(value, axis, bit):
    return lax.ppermute(value, axis, [(i, i ^ bit) for i in range(2 if axis == "core" else RING)])


def dot_last(left, right):
    return lax.dot_general(left, right, (((1,), (1,)), ((), ())), preferred_element_type=jnp.float32)


def dot_first(left, right):
    return lax.dot_general(left, right, (((0,), (0,)), ((), ())), preferred_element_type=jnp.float32)


def around(value, axis):
    return [value] + [shift(value, axis, s) for s in STEPS[1:]]


def ring_reduce(lefts, right, axis):
    up, down, near, own = (dot_last(left, right).astype(jnp.bfloat16) for left in lefts)
    half = own.shape[0] // 2
    wide = lambda v: v.astype(jnp.float32)
    up = shift(up, axis, 1)
    down = shift(down, axis, -1)
    sum_up = shift((wide(near[:half]) + wide(up[:half])).astype(jnp.bfloat16), axis, 1)
    sum_down = shift((wide(near[half:]) + wide(down[:half])).astype(jnp.bfloat16), axis, -1)
    top = wide(own[:half]) + wide(down[half:]) + wide(sum_up)
    bottom = wide(own[half:]) + wide(up[half:]) + wide(sum_down)
    return jnp.concatenate([top, bottom], axis=0)


ANY = pl.BlockSpec(memory_space=pl.ANY)
SMEM = pl.BlockSpec(memory_space=pltpu.SMEM)
VMEM = pl.BlockSpec(memory_space=pltpu.VMEM)


def call(kernel, name, inputs, after, outs, cost, limit, scratch=(), aliases=None, in_specs=None, out_specs=None):
    count = len(inputs)

    def body(*refs):
        kernel(*refs[:count], *refs[count + len(after) :])

    return pl.pallas_call(
        body,
        in_specs=(in_specs or [VMEM] * count) + [ANY] * len(after),
        out_specs=out_specs or [VMEM] * len(outs),
        out_shape=outs,
        scratch_shapes=list(scratch),
        input_output_aliases=aliases or {},
        compiler_params=pltpu.CompilerParams(vmem_limit_bytes=limit * MIB),
        cost_estimate=cost,
        name=name,
    )(*inputs, *after)


def gate_kernel(weight_ref, out_ref, gate_ref, up_ref, *rest):
    grad_ref = rest[-1]
    hidden_grad = dot_last(weight_ref[...], out_ref[...])
    gate = gate_ref[...].astype(jnp.float32)
    sigma = 1.0 / (1.0 + jnp.exp(-gate))
    slope = sigma * (1.0 + gate * (1.0 - sigma))
    grad_ref[...] = (hidden_grad * up_ref[...].astype(jnp.float32) * slope).astype(grad_ref.dtype)


def gate_gradient(weight, out_grad, gate, up, after, rows):
    width, depth = weight.shape
    tokens = out_grad.shape[0]
    block = pl.BlockSpec((rows, tokens), lambda i: (i, 0))
    return pl.pallas_call(
        gate_kernel,
        grid=(width // rows,),
        in_specs=[
            pl.BlockSpec((rows, depth), lambda i: (i, 0)),
            pl.BlockSpec((tokens, depth), lambda i: (0, 0)),
            block,
            block,
        ]
        + [pl.BlockSpec(memory_space=pl.ANY)] * len(after),
        out_specs=block,
        out_shape=jax.ShapeDtypeStruct((width, tokens), jnp.bfloat16),
        compiler_params=pltpu.CompilerParams(vmem_limit_bytes=50 * MIB),
        cost_estimate=HEAVY,
        name="gate_gradient",
    )(weight, out_grad, gate, up, *after)


def squares_kernel(out_ref, act_ref, hidden_ref, gate_ref, total_ref):
    down = jnp.sum(dot_first(hidden_ref[...], hidden_ref[...]) * dot_last(out_ref[...], out_ref[...]))
    gate = jnp.sum(dot_first(gate_ref[...], gate_ref[...]) * dot_last(act_ref[...], act_ref[...]))
    row = lax.broadcasted_iota(jnp.int32, total_ref.shape, 0)
    total_ref[...] = jnp.where(row < RING, down, gate)


def factor_kernel(*refs):
    total = refs[0][...] + refs[1][...] + refs[2][...] + refs[3][...]
    row = lax.broadcasted_iota(jnp.int32, total.shape, 0)
    radius = jnp.where(row < RING, refs[4][0], refs[4][1])
    refs[5][...] = radius / jnp.maximum(jnp.sqrt(total), radius)
    refs[6][...] = jnp.ones_like(refs[6])


def stack_kernel(*refs):
    blocks, wide_ref = refs[:RING], refs[-1]
    for at, block in enumerate(blocks):
        wide_ref[at] = block[...]


def stacked(blocks, after):
    rows, tokens = blocks[0].shape
    steps = 4
    return pl.pallas_call(
        stack_kernel,
        grid=(steps,),
        in_specs=[pl.BlockSpec((rows // steps, tokens), lambda i: (i, 0))] * RING + [ANY] * len(after),
        out_specs=pl.BlockSpec((RING, rows // steps, tokens), lambda i: (0, i, 0)),
        out_shape=jax.ShapeDtypeStruct((RING, rows, tokens), blocks[0].dtype),
        compiler_params=pltpu.CompilerParams(vmem_limit_bytes=6 * MIB),
        cost_estimate=SMALL,
        name="stack",
    )(*blocks, *after)


def lefts_kernel(owner, goal_ref, mine_ref, other_ref, *refs):
    factors, outs, held_ref, sems = refs[:RING], refs[RING : 2 * RING], refs[-2], refs[-1]
    rows, tokens = outs[0].shape[0], mine_ref.shape[2]
    half = rows // 2
    far, after, before, own = range(4)
    halves = ((far, 0), (after, 1), (far, 1), (before, 0), (after, 0), (before, 1), (own, 0), (own, 1))
    waits = []
    for source, here in ((mine_ref, goal_ref[0] == owner), (other_ref, goal_ref[0] != owner)):
        copies = []
        for at, (goal, part) in enumerate(halves):
            start = pl.multiple_of(goal_ref[1 + goal] * rows + part * half, 16)
            for block in range(RING):
                lanes = pl.ds(block * tokens, tokens)
                target = held_ref.at[at // 2, pl.ds(at % 2 * half, half), lanes]
                copies.append(pltpu.make_async_copy(source.at[block, pl.ds(start, half), :], target, sems.at[at, block]))

        @pl.when(here)
        def _():
            for copy in copies:
                copy.start()

        waits = copies
    scale = jnp.concatenate([f[pl.ds(owner * RING, 1), :] for f in factors for _ in range(tokens // LANES)], axis=1)
    for at, out in enumerate(outs):
        for copy in waits[at * 2 * RING : (at + 1) * 2 * RING]:
            copy.wait()
        out[...] = (held_ref[at].astype(jnp.float32) * scale).astype(out.dtype)


def lefts_of(owner, goals, mine, other, factors, after):
    blocks, depth, tokens = mine.shape
    shape = (depth // RING, blocks * tokens)
    return call(
        functools.partial(lefts_kernel, owner),
        "lefts",
        [goals, mine, other, *factors],
        after,
        [jax.ShapeDtypeStruct(shape, mine.dtype)] * RING,
        SMALL,
        10,
        [pltpu.VMEM((RING, *shape), mine.dtype), pltpu.SemaphoreType.DMA((2 * RING, RING))],
        None,
        [SMEM, ANY, ANY] + [VMEM] * RING,
    )


def parts_kernel(place_ref, out_ref, act_ref, *refs):
    targets, window_ref, sems = refs[:RING], refs[RING], refs[RING + 1]
    rows, tokens = targets[0].shape
    owned = rows // RING
    for at in range(RING):
        place = place_ref[1 + at]

        @pl.when(place_ref[0] == 0)
        def _():
            lanes = pl.ds(pl.multiple_of(place * rows, LANES), rows)
            pltpu.make_async_copy(out_ref.at[:, lanes], window_ref.at[at], sems.at[at]).start()

        @pl.when(place_ref[0] != 0)
        def _():
            lanes = pl.ds(at * rows, rows)
            pltpu.make_async_copy(act_ref.at[:, lanes], window_ref.at[at], sems.at[at]).start()

    for at in range(RING):
        pltpu.make_async_copy(out_ref.at[:, pl.ds(0, rows)], window_ref.at[at], sems.at[at]).wait()
    for at in range(RING):
        turned = window_ref[at].T

        @pl.when(place_ref[0] == 0)
        def _():
            targets[at][...] = turned

        @pl.when(place_ref[0] != 0)
        def _():
            for goal in range(RING):
                for place in range(RING):

                    @pl.when(place_ref[1 + goal] == place)
                    def _():
                        targets[goal][pl.ds(at * owned, owned), :] = turned[place * owned : (place + 1) * owned]


def column_parts(out_grad, activations, places, after):
    tokens, depth = out_grad.shape
    rows = depth // RING
    return call(
        parts_kernel,
        "column_parts",
        [places, out_grad, activations],
        after,
        [jax.ShapeDtypeStruct((rows, tokens), out_grad.dtype)] * RING,
        SMALL,
        16,
        [pltpu.VMEM((RING, tokens, rows), out_grad.dtype), pltpu.SemaphoreType.DMA((RING,))],
        None,
        [SMEM, ANY, ANY],
    )


def local(activations, out_grad, gate_pre, up_pre, down_weight, clip_bounds):
    tokens, model_width = activations.shape
    full_hidden = gate_pre.shape[1] * RING * CORES
    example_total = RING * RING
    at_x, at_y, at_core = (lax.axis_index(a) for a in ("x", "y", "core"))

    gate, up = gate_pre.T, up_pre.T
    gate_val = gate.astype(jnp.float32)
    hidden = (jax.nn.silu(gate_val) * up.astype(jnp.float32)).astype(jnp.bfloat16)
    place = jnp.where(at_core == 0, at_x, at_y)
    parts = column_parts(out_grad, activations, jnp.stack([at_core] + [(place + s) % RING for s in STEPS]), [hidden])
    parts_here = [parts[0], *(shift(p, "spread", s) for p, s in zip(parts[1:], STEPS[1:], strict=True))]
    gate_grad = gate_gradient(down_weight.T, out_grad, gate, up, [hidden, parts[0]], 288)
    hidden_blocks, gate_blocks = around(hidden, "x"), around(gate_grad, "y")

    small = jax.ShapeDtypeStruct((2 * RING, LANES), jnp.float32)
    (squares,) = call(squares_kernel, "squares", [out_grad, activations, hidden, gate_grad], parts_here[1:], [small], SMALL, 10)
    sums = around(squares + swap(squares, "core", 1), "z")
    mine = stacked(parts_here, sums[1:])
    radius = clip_bounds * math.sqrt(float(model_width * full_hidden * SEQ))
    factor, unit = call(
        factor_kernel,
        "factor",
        [*sums, radius],
        [*hidden_blocks[1:3], *gate_blocks[1:3], mine],
        [small, jax.ShapeDtypeStruct((1, 1), jnp.float32)],
        SMALL,
        1,
        in_specs=[VMEM] * 4 + [SMEM],
    )
    other = swap(mine, "core", 1)
    far = [hidden_blocks[3], gate_blocks[3]]
    goals_of = lambda at: jnp.stack([at_core] + [(at + s) % RING for s in (2, 1, -1, 0)])
    along_x, along_y = around(factor, "x"), around(factor, "y")
    gate_lefts = lefts_of(1, goals_of(at_x), mine, other, along_y, [*far, *along_x[1:]])
    down_lefts = lefts_of(0, goals_of(at_y), mine, other, along_x, far)

    def wide(blocks):
        return jnp.concatenate([(unit * b.astype(jnp.float32)).astype(jnp.bfloat16) for b in blocks], axis=1)

    down = ring_reduce(down_lefts, wide(hidden_blocks), "y")
    gated = ring_reduce(gate_lefts, wide(gate_blocks), "x")
    return ((down / example_total).astype(jnp.bfloat16), (gated / example_total).astype(jnp.bfloat16))


def solution(mesh):
    torus = Mesh(mesh.devices.reshape(RING, RING, RING, 2), ("x", "y", "z", "core"))
    dp, tensor = ("x", "y"), ("z", "core")
    in_specs = (P(dp, None), P(dp, None), P(dp, tensor), P(dp, tensor), P(None, tensor), P())
    out_specs = (P(dp, tensor), P(dp, tensor))
    return jax.shard_map(local, mesh=torus, in_specs=in_specs, out_specs=out_specs, check_vma=False)
```

```python
import functools
import math

import jax
import jax.numpy as jnp
from jax import lax
from jax.experimental import pallas as pl
from jax.experimental.pallas import tpu as pltpu
from jax.sharding import Mesh, PartitionSpec as P

SEQ = 256
RING = 4
CORES = 2
STEPS = (0, 1, -1, 2)
LANES = 128
MIB = 1024 * 1024
HEAVY = pl.CostEstimate(flops=10**12, bytes_accessed=10**9, transcendentals=0)
SMALL = pl.CostEstimate(flops=0, bytes_accessed=0, transcendentals=0)


def move(value, axes, goal):
    pairs = []
    for x in range(RING):
        for y in range(RING):
            for core in range(2):
                to_x, to_y = goal(x, y, core)
                pairs.append(((x * RING + y) * 2 + core, (to_x % RING * RING + to_y % RING) * 2 + core))
    return lax.ppermute(value, axes, pairs)


def shift(value, axis, step):
    if axis != "spread":
        return lax.ppermute(value, axis, [(i, (i + step) % RING) for i in range(RING)])
    pairs = []
    for x in range(RING):
        for y in range(RING):
            for core in range(2):
                to_x, to_y = ((x + step) % RING, y) if core == 0 else (x, (y + step) % RING)
                pairs.append(((x * RING + y) * 2 + core, (to_x * RING + to_y) * 2 + core))
    return lax.ppermute(value, ("x", "y", "core"), pairs)


def swap(value, axis, bit):
    return lax.ppermute(value, axis, [(i, i ^ bit) for i in range(2 if axis == "core" else RING)])


def dot_last(left, right):
    return lax.dot_general(left, right, (((1,), (1,)), ((), ())), preferred_element_type=jnp.float32)


def dot_first(left, right):
    return lax.dot_general(left, right, (((0,), (0,)), ((), ())), preferred_element_type=jnp.float32)


def around(value, axis):
    return [value] + [shift(value, axis, s) for s in STEPS[1:]]


def ring_reduce(lefts, right, axis):
    up, down, near, own = (dot_last(left, right).astype(jnp.bfloat16) for left in lefts)
    half = own.shape[0] // 2
    wide = lambda v: v.astype(jnp.float32)
    up = shift(up, axis, 1)
    down = shift(down, axis, -1)
    sum_up = shift((wide(near[:half]) + wide(up[:half])).astype(jnp.bfloat16), axis, 1)
    sum_down = shift((wide(near[half:]) + wide(down[:half])).astype(jnp.bfloat16), axis, -1)
    top = wide(own[:half]) + wide(down[half:]) + wide(sum_up)
    bottom = wide(own[half:]) + wide(up[half:]) + wide(sum_down)
    return jnp.concatenate([top, bottom], axis=0)


ANY = pl.BlockSpec(memory_space=pl.ANY)
SMEM = pl.BlockSpec(memory_space=pltpu.SMEM)
VMEM = pl.BlockSpec(memory_space=pltpu.VMEM)


def call(kernel, name, inputs, after, outs, cost, limit, scratch=(), aliases=None, in_specs=None, out_specs=None):
    count = len(inputs)

    def body(*refs):
        kernel(*refs[:count], *refs[count + len(after) :])

    return pl.pallas_call(
        body,
        in_specs=(in_specs or [VMEM] * count) + [ANY] * len(after),
        out_specs=out_specs or [VMEM] * len(outs),
        out_shape=outs,
        scratch_shapes=list(scratch),
        input_output_aliases=aliases or {},
        compiler_params=pltpu.CompilerParams(vmem_limit_bytes=limit * MIB),
        cost_estimate=cost,
        name=name,
    )(*inputs, *after)


def gate_kernel(weight_ref, out_ref, gate_ref, up_ref, *rest):
    hidden_ref, grad_ref = rest[-2:]
    gate = gate_ref[...].astype(jnp.float32)
    up = up_ref[...].astype(jnp.float32)
    sigma = 1.0 / (1.0 + jnp.exp(-gate))
    hidden_ref[...] = (gate * sigma * up).astype(hidden_ref.dtype)
    hidden_grad = dot_last(weight_ref[...], out_ref[...])
    grad_ref[...] = (hidden_grad * up * (sigma * (1.0 + gate * (1.0 - sigma)))).astype(grad_ref.dtype)


def hidden_and_gradient(weight, out_grad, gate, up, after, rows):
    width, depth = weight.shape
    tokens = out_grad.shape[0]
    block = pl.BlockSpec((rows, tokens), lambda i: (i, 0))
    shape = jax.ShapeDtypeStruct((width, tokens), jnp.bfloat16)
    return pl.pallas_call(
        gate_kernel,
        grid=(width // rows,),
        in_specs=[
            pl.BlockSpec((rows, depth), lambda i: (i, 0)),
            pl.BlockSpec((tokens, depth), lambda i: (0, 0)),
            block,
            block,
        ]
        + [ANY] * len(after),
        out_specs=[block, block],
        out_shape=[shape, shape],
        compiler_params=pltpu.CompilerParams(vmem_limit_bytes=50 * MIB),
        cost_estimate=HEAVY,
        name="hidden_and_gradient",
    )(weight, out_grad, gate, up, *after)


def squares_kernel(out_ref, act_ref, hidden_ref, gate_ref, total_ref):
    down = jnp.sum(dot_first(hidden_ref[...], hidden_ref[...]) * dot_last(out_ref[...], out_ref[...]))
    gate = jnp.sum(dot_first(gate_ref[...], gate_ref[...]) * dot_last(act_ref[...], act_ref[...]))
    row = lax.broadcasted_iota(jnp.int32, total_ref.shape, 0)
    total_ref[...] = jnp.where(row < RING, down, gate)


def copy_kernel(source_ref, target_ref):
    target_ref[...] = source_ref[...]


def pack_kernel(*refs):
    for at in range(RING - 1):
        refs[RING + 1][at] = refs[at][...]


def factor_kernel(unit, *refs):
    total = refs[0][...] + refs[1][...] + refs[2][...] + refs[3][...]
    row = lax.broadcasted_iota(jnp.int32, total.shape, 0)
    radius = jnp.where(row < RING, refs[4][0], refs[4][1]) * unit
    refs[5][...] = radius / jnp.maximum(jnp.sqrt(total), radius)


def wide_kernel(*refs):
    tokens = refs[0].shape[1]
    for at in range(RING):
        refs[RING][:, pl.ds(at * tokens, tokens)] = refs[at][...]


def wide(blocks, after):
    rows, tokens = blocks[0].shape
    shape = jax.ShapeDtypeStruct((rows, RING * tokens), blocks[0].dtype)
    return call(wide_kernel, "wide", blocks, after, [shape], SMALL, 12)[0]


def stack_kernel(*refs):
    blocks, wide_ref = refs[:RING], refs[-1]
    for at, block in enumerate(blocks):
        wide_ref[at] = block[...]


def stacked(blocks, after):
    rows, tokens = blocks[0].shape
    steps = 4
    return pl.pallas_call(
        stack_kernel,
        grid=(steps,),
        in_specs=[pl.BlockSpec((rows // steps, tokens), lambda i: (i, 0))] * RING + [ANY] * len(after),
        out_specs=pl.BlockSpec((RING, rows // steps, tokens), lambda i: (0, i, 0)),
        out_shape=jax.ShapeDtypeStruct((RING, rows, tokens), blocks[0].dtype),
        compiler_params=pltpu.CompilerParams(vmem_limit_bytes=6 * MIB),
        cost_estimate=SMALL,
        name="stack",
    )(*blocks, *after)


def lefts_kernel(owner, axis, mine_ref, other_ref, *refs):
    factor_ref, mine_factors, other_factors = refs[:3]
    outs, held_ref, sems = refs[3 : 3 + RING], refs[-2], refs[-1]
    rows, tokens = outs[0].shape[0], mine_ref.shape[2]
    half = rows // 2
    core, at_axis = lax.axis_index("core"), lax.axis_index(axis)
    far, after, before, own = 2, 1, RING - 1, 0
    halves = ((far, 0), (after, 1), (far, 1), (before, 0), (after, 0), (before, 1), (own, 0), (own, 1))
    waits = []
    for source, here in ((mine_ref, core == owner), (other_ref, core != owner)):
        copies = []
        for at, (goal, part) in enumerate(halves):
            start = pl.multiple_of(lax.rem(at_axis + goal, RING) * rows + part * half, 16)
            for block in range(RING):
                lanes = pl.ds(block * tokens, tokens)
                target = held_ref.at[at // 2, pl.ds(at % 2 * half, half), lanes]
                copies.append(pltpu.make_async_copy(source.at[block, pl.ds(start, half), :], target, sems.at[at, block]))

        @pl.when(here)
        def _():
            for copy in copies:
                copy.start()

        waits = copies
    line = pl.ds(owner * RING, 1)
    scales = [factor_ref[line, :]]
    for at in range(RING - 1):
        scales.append(jnp.where(core == owner, mine_factors[at, line, :], other_factors[at, line, :]))
    scale = jnp.concatenate([f for f in scales for _ in range(tokens // LANES)], axis=1)
    for at, out in enumerate(outs):
        for copy in waits[at * 2 * RING : (at + 1) * 2 * RING]:
            copy.wait()
        out[...] = (held_ref[at].astype(jnp.float32) * scale).astype(out.dtype)


def lefts_of(owner, axis, mine, other, factors):
    blocks, depth, tokens = mine.shape
    shape = (depth // RING, blocks * tokens)
    return call(
        functools.partial(lefts_kernel, owner, axis),
        "lefts",
        [mine, other, *factors],
        [],
        [jax.ShapeDtypeStruct(shape, mine.dtype)] * RING,
        SMALL,
        10,
        [pltpu.VMEM((RING, *shape), mine.dtype), pltpu.SemaphoreType.DMA((2 * RING, RING))],
        None,
        [ANY, ANY] + [VMEM] * 3,
    )


def parts_kernel(out_ref, act_ref, *refs):
    targets, window_ref, sems = refs[:RING], refs[RING], refs[RING + 1]
    rows, tokens = targets[0].shape
    owned = rows // RING
    core = lax.axis_index("core")
    at_place = jnp.where(core == 0, lax.axis_index("x"), lax.axis_index("y"))
    places = [lax.rem(at_place + s + RING, RING) for s in STEPS]
    for at in range(RING):
        place = places[at]

        @pl.when(core == 0)
        def _():
            lanes = pl.ds(pl.multiple_of(place * rows, LANES), rows)
            pltpu.make_async_copy(out_ref.at[:, lanes], window_ref.at[at], sems.at[at]).start()

        @pl.when(core != 0)
        def _():
            lanes = pl.ds(at * rows, rows)
            pltpu.make_async_copy(act_ref.at[:, lanes], window_ref.at[at], sems.at[at]).start()

    for at in range(RING):
        pltpu.make_async_copy(out_ref.at[:, pl.ds(0, rows)], window_ref.at[at], sems.at[at]).wait()
    for at in range(RING):
        turned = window_ref[at].T

        @pl.when(core == 0)
        def _():
            targets[at][...] = turned

        @pl.when(core != 0)
        def _():
            for goal in range(RING):
                for place in range(RING):

                    @pl.when(places[goal] == place)
                    def _():
                        targets[goal][pl.ds(at * owned, owned), :] = turned[place * owned : (place + 1) * owned]


def column_parts(out_grad, activations):
    tokens, depth = out_grad.shape
    rows = depth // RING
    return call(
        parts_kernel,
        "column_parts",
        [out_grad, activations],
        [],
        [jax.ShapeDtypeStruct((rows, tokens), out_grad.dtype)] * RING,
        SMALL,
        16,
        [pltpu.VMEM((RING, tokens, rows), out_grad.dtype), pltpu.SemaphoreType.DMA((RING,))],
        None,
        [ANY, ANY],
    )


def local(activations, out_grad, gate_pre, up_pre, down_weight, clip_bounds):
    tokens, model_width = activations.shape
    full_hidden = gate_pre.shape[1] * RING * CORES
    example_total = RING * RING

    parts = column_parts(out_grad, activations)
    parts_here = [parts[0], *(shift(p, "spread", s) for p, s in zip(parts[1:], STEPS[1:], strict=True))]
    hidden, gate_grad = hidden_and_gradient(down_weight.T, out_grad, gate_pre.T, up_pre.T, [parts[0]], 288)
    near_hidden = [shift(hidden, "x", s) for s in STEPS[1:3]]
    near_gate = [shift(gate_grad, "y", s) for s in STEPS[1:3]]

    small = jax.ShapeDtypeStruct((2 * RING, LANES), jnp.float32)
    mine = stacked(parts_here, [gate_grad])
    other = swap(mine, "core", 1)
    (squares,) = call(
        squares_kernel, "squares", [out_grad, activations, hidden, gate_grad], parts_here[1:], [small], HEAVY, 10
    )
    (squares,) = call(copy_kernel, "held", [squares], [other], [small], SMALL, 1)
    sums = around(squares + swap(squares, "core", 1), "z")
    (factor,) = call(
        functools.partial(factor_kernel, math.sqrt(float(model_width * full_hidden * SEQ))),
        "factor",
        [*sums, clip_bounds],
        [*near_hidden, *near_gate],
        [small],
        SMALL,
        1,
        in_specs=[VMEM] * 4 + [SMEM],
    )
    mine_factors, hidden, gate_grad = call(
        pack_kernel,
        "pack",
        [*(shift(factor, "spread", s) for s in STEPS[1:]), hidden, gate_grad],
        [],
        [
            jax.ShapeDtypeStruct((RING - 1, *small.shape), jnp.float32),
            *(jax.ShapeDtypeStruct(v.shape, v.dtype) for v in (hidden, gate_grad)),
        ],
        SMALL,
        1,
        (),
        {RING - 1: 1, RING: 2},
        [VMEM] * (RING - 1) + [ANY] * 2,
        [VMEM] + [ANY] * 2,
    )
    hidden_blocks = [hidden, *near_hidden, shift(hidden, "x", 2)]
    gate_blocks = [gate_grad, *near_gate, shift(gate_grad, "y", 2)]
    factors = [factor, mine_factors, swap(mine_factors, "core", 1)]
    gate_lefts = lefts_of(1, "x", mine, other, factors)
    down_lefts = lefts_of(0, "y", mine, other, factors)
    down = ring_reduce(down_lefts, wide(hidden_blocks, []), "y")
    gated = ring_reduce(gate_lefts, wide(gate_blocks, []), "x")
    return ((down / example_total).astype(jnp.bfloat16), (gated / example_total).astype(jnp.bfloat16))


def solution(mesh):
    torus = Mesh(mesh.devices.reshape(RING, RING, RING, 2), ("x", "y", "z", "core"))
    dp, tensor = ("x", "y"), ("z", "core")
    in_specs = (P(dp, None), P(dp, None), P(dp, tensor), P(dp, tensor), P(None, tensor), P())
    out_specs = (P(dp, tensor), P(dp, tensor))
    return jax.shard_map(local, mesh=torus, in_specs=in_specs, out_specs=out_specs, check_vma=False)
```

```python
import functools
import math

import jax
import jax.numpy as jnp
from jax import lax
from jax.experimental import pallas as pl
from jax.experimental.pallas import tpu as pltpu
from jax.sharding import Mesh, PartitionSpec as P

SEQ = 256
RING = 4
CORES = 2
STEPS = (0, 1, -1, 2)
LANES = 128
MIB = 1024 * 1024
HEAVY = pl.CostEstimate(flops=10**12, bytes_accessed=10**9, transcendentals=0)
SMALL = pl.CostEstimate(flops=0, bytes_accessed=0, transcendentals=0)


def move(value, axes, goal):
    pairs = []
    for x in range(RING):
        for y in range(RING):
            for core in range(2):
                to_x, to_y = goal(x, y, core)
                pairs.append(((x * RING + y) * 2 + core, (to_x % RING * RING + to_y % RING) * 2 + core))
    return lax.ppermute(value, axes, pairs)


def shift(value, axis, step):
    if axis != "spread":
        return lax.ppermute(value, axis, [(i, (i + step) % RING) for i in range(RING)])
    pairs = []
    for x in range(RING):
        for y in range(RING):
            for core in range(2):
                to_x, to_y = ((x + step) % RING, y) if core == 0 else (x, (y + step) % RING)
                pairs.append(((x * RING + y) * 2 + core, (to_x * RING + to_y) * 2 + core))
    return lax.ppermute(value, ("x", "y", "core"), pairs)


def swap(value, axis, bit):
    return lax.ppermute(value, axis, [(i, i ^ bit) for i in range(2 if axis == "core" else RING)])


def dot_last(left, right):
    return lax.dot_general(left, right, (((1,), (1,)), ((), ())), preferred_element_type=jnp.float32)


def dot_first(left, right):
    return lax.dot_general(left, right, (((0,), (0,)), ((), ())), preferred_element_type=jnp.float32)


def around(value, axis):
    return [value] + [shift(value, axis, s) for s in STEPS[1:]]


def ring_reduce(lefts, right, axis):
    up, down, near, own = (dot_last(left, right).astype(jnp.bfloat16) for left in lefts)
    half = own.shape[0] // 2
    wide = lambda v: v.astype(jnp.float32)
    up = shift(up, axis, 1)
    down = shift(down, axis, -1)
    sum_up = shift((wide(near[:half]) + wide(up[:half])).astype(jnp.bfloat16), axis, 1)
    sum_down = shift((wide(near[half:]) + wide(down[:half])).astype(jnp.bfloat16), axis, -1)
    top = wide(own[:half]) + wide(down[half:]) + wide(sum_up)
    bottom = wide(own[half:]) + wide(up[half:]) + wide(sum_down)
    return jnp.concatenate([top, bottom], axis=0)


ANY = pl.BlockSpec(memory_space=pl.ANY)
SMEM = pl.BlockSpec(memory_space=pltpu.SMEM)
VMEM = pl.BlockSpec(memory_space=pltpu.VMEM)


def call(kernel, name, inputs, after, outs, cost, limit, scratch=(), aliases=None, in_specs=None, out_specs=None):
    count = len(inputs)

    def body(*refs):
        kernel(*refs[:count], *refs[count + len(after) :])

    return pl.pallas_call(
        body,
        in_specs=(in_specs or [VMEM] * count) + [ANY] * len(after),
        out_specs=out_specs or [VMEM] * len(outs),
        out_shape=outs,
        scratch_shapes=list(scratch),
        input_output_aliases=aliases or {},
        compiler_params=pltpu.CompilerParams(vmem_limit_bytes=limit * MIB),
        cost_estimate=cost,
        name=name,
    )(*inputs, *after)


def gate_kernel(weight_ref, out_ref, gate_ref, up_ref, *rest):
    hidden_ref, grad_ref = rest[-2:]
    gate = gate_ref[...].astype(jnp.float32)
    up = up_ref[...].astype(jnp.float32)
    sigma = 1.0 / (1.0 + jnp.exp(-gate))
    hidden_ref[...] = (gate * sigma * up).astype(hidden_ref.dtype)
    hidden_grad = dot_last(weight_ref[...], out_ref[...])
    grad_ref[...] = (hidden_grad * up * (sigma * (1.0 + gate * (1.0 - sigma)))).astype(grad_ref.dtype)


def hidden_and_gradient(weight, out_grad, gate, up, after, rows):
    width, depth = weight.shape
    tokens = out_grad.shape[0]
    block = pl.BlockSpec((rows, tokens), lambda i: (i, 0))
    shape = jax.ShapeDtypeStruct((width, tokens), jnp.bfloat16)
    return pl.pallas_call(
        gate_kernel,
        grid=(width // rows,),
        in_specs=[
            pl.BlockSpec((rows, depth), lambda i: (i, 0)),
            pl.BlockSpec((tokens, depth), lambda i: (0, 0)),
            block,
            block,
        ]
        + [ANY] * len(after),
        out_specs=[block, block],
        out_shape=[shape, shape],
        compiler_params=pltpu.CompilerParams(vmem_limit_bytes=50 * MIB),
        cost_estimate=HEAVY,
        name="hidden_and_gradient",
    )(weight, out_grad, gate, up, *after)


def squares_kernel(out_ref, act_ref, hidden_ref, gate_ref, total_ref):
    down = jnp.sum(dot_first(hidden_ref[...], hidden_ref[...]) * dot_last(out_ref[...], out_ref[...]))
    gate = jnp.sum(dot_first(gate_ref[...], gate_ref[...]) * dot_last(act_ref[...], act_ref[...]))
    row = lax.broadcasted_iota(jnp.int32, total_ref.shape, 0)
    total_ref[...] = jnp.where(row < RING, down, gate)


def copy_kernel(source_ref, target_ref):
    target_ref[...] = source_ref[...]


def pack_kernel(*refs):
    for at in range(RING - 1):
        refs[RING + 1][at] = refs[at][...]


def factor_kernel(unit, *refs):
    total = refs[0][...] + refs[1][...]
    row = lax.broadcasted_iota(jnp.int32, total.shape, 0)
    radius = jnp.where(row < RING, refs[2][0], refs[2][1]) * unit
    refs[3][...] = radius / jnp.maximum(jnp.sqrt(total), radius)


def wide_kernel(*refs):
    tokens = refs[0].shape[1]
    for at in range(RING):
        refs[RING][:, pl.ds(at * tokens, tokens)] = refs[at][...]


def wide(blocks, after):
    rows, tokens = blocks[0].shape
    shape = jax.ShapeDtypeStruct((rows, RING * tokens), blocks[0].dtype)
    return call(wide_kernel, "wide", blocks, after, [shape], SMALL, 12)[0]


def stack_kernel(*refs):
    blocks, wide_ref = refs[:RING], refs[-1]
    for at, block in enumerate(blocks):
        wide_ref[at] = block[...]


def stacked(blocks, after):
    rows, tokens = blocks[0].shape
    steps = 4
    return pl.pallas_call(
        stack_kernel,
        grid=(steps,),
        in_specs=[pl.BlockSpec((rows // steps, tokens), lambda i: (i, 0))] * RING + [ANY] * len(after),
        out_specs=pl.BlockSpec((RING, rows // steps, tokens), lambda i: (0, i, 0)),
        out_shape=jax.ShapeDtypeStruct((RING, rows, tokens), blocks[0].dtype),
        compiler_params=pltpu.CompilerParams(vmem_limit_bytes=6 * MIB),
        cost_estimate=SMALL,
        name="stack",
    )(*blocks, *after)


def lefts_kernel(owner, axis, mine_ref, other_ref, *refs):
    factor_ref, mine_factors, other_factors = refs[:3]
    outs, held_ref, sems = refs[3 : 3 + RING], refs[-2], refs[-1]
    rows, tokens = outs[0].shape[0], mine_ref.shape[2]
    half = rows // 2
    core, at_axis = lax.axis_index("core"), lax.axis_index(axis)
    far, after, before, own = 2, 1, RING - 1, 0
    halves = ((far, 0), (after, 1), (far, 1), (before, 0), (after, 0), (before, 1), (own, 0), (own, 1))
    waits = []
    for source, here in ((mine_ref, core == owner), (other_ref, core != owner)):
        copies = []
        for at, (goal, part) in enumerate(halves):
            start = pl.multiple_of(lax.rem(at_axis + goal, RING) * rows + part * half, 16)
            for block in range(RING):
                lanes = pl.ds(block * tokens, tokens)
                target = held_ref.at[at // 2, pl.ds(at % 2 * half, half), lanes]
                copies.append(pltpu.make_async_copy(source.at[block, pl.ds(start, half), :], target, sems.at[at, block]))

        @pl.when(here)
        def _():
            for copy in copies:
                copy.start()

        waits = copies
    line = pl.ds(owner * RING, 1)
    scales = [factor_ref[line, :]]
    for at in range(RING - 1):
        scales.append(jnp.where(core == owner, mine_factors[at, line, :], other_factors[at, line, :]))
    scale = jnp.concatenate([f for f in scales for _ in range(tokens // LANES)], axis=1)
    for at, out in enumerate(outs):
        for copy in waits[at * 2 * RING : (at + 1) * 2 * RING]:
            copy.wait()
        out[...] = (held_ref[at].astype(jnp.float32) * scale).astype(out.dtype)


def lefts_of(owner, axis, mine, other, factors):
    blocks, depth, tokens = mine.shape
    shape = (depth // RING, blocks * tokens)
    return call(
        functools.partial(lefts_kernel, owner, axis),
        "lefts",
        [mine, other, *factors],
        [],
        [jax.ShapeDtypeStruct(shape, mine.dtype)] * RING,
        SMALL,
        10,
        [pltpu.VMEM((RING, *shape), mine.dtype), pltpu.SemaphoreType.DMA((2 * RING, RING))],
        None,
        [ANY, ANY] + [VMEM] * 3,
    )


def parts_kernel(out_ref, act_ref, *refs):
    targets, window_ref, sems = refs[:RING], refs[RING], refs[RING + 1]
    rows, tokens = targets[0].shape
    owned = rows // RING
    core = lax.axis_index("core")
    at_place = jnp.where(core == 0, lax.axis_index("x"), lax.axis_index("y"))
    places = [lax.rem(at_place + s + RING, RING) for s in STEPS]
    for at in range(RING):
        place = places[at]

        @pl.when(core == 0)
        def _():
            lanes = pl.ds(pl.multiple_of(place * rows, LANES), rows)
            pltpu.make_async_copy(out_ref.at[:, lanes], window_ref.at[at], sems.at[at]).start()

        @pl.when(core != 0)
        def _():
            lanes = pl.ds(at * rows, rows)
            pltpu.make_async_copy(act_ref.at[:, lanes], window_ref.at[at], sems.at[at]).start()

    for at in range(RING):
        pltpu.make_async_copy(out_ref.at[:, pl.ds(0, rows)], window_ref.at[at], sems.at[at]).wait()
    for at in range(RING):
        turned = window_ref[at].T

        @pl.when(core == 0)
        def _():
            targets[at][...] = turned

        @pl.when(core != 0)
        def _():
            for goal in range(RING):
                for place in range(RING):

                    @pl.when(places[goal] == place)
                    def _():
                        targets[goal][pl.ds(at * owned, owned), :] = turned[place * owned : (place + 1) * owned]


def column_parts(out_grad, activations):
    tokens, depth = out_grad.shape
    rows = depth // RING
    return call(
        parts_kernel,
        "column_parts",
        [out_grad, activations],
        [],
        [jax.ShapeDtypeStruct((rows, tokens), out_grad.dtype)] * RING,
        SMALL,
        16,
        [pltpu.VMEM((RING, tokens, rows), out_grad.dtype), pltpu.SemaphoreType.DMA((RING,))],
        None,
        [ANY, ANY],
    )


def local(activations, out_grad, gate_pre, up_pre, down_weight, clip_bounds):
    tokens, model_width = activations.shape
    full_hidden = gate_pre.shape[1] * RING * CORES
    example_total = RING * RING

    parts = column_parts(out_grad, activations)
    parts_here = [parts[0], *(shift(p, "spread", s) for p, s in zip(parts[1:], STEPS[1:], strict=True))]
    hidden, gate_grad = hidden_and_gradient(down_weight.T, out_grad, gate_pre.T, up_pre.T, [parts[0]], 864)
    near_hidden = [shift(hidden, "x", s) for s in STEPS[1:3]]
    near_gate = [shift(gate_grad, "y", s) for s in STEPS[1:3]]

    small = jax.ShapeDtypeStruct((2 * RING, LANES), jnp.float32)
    mine = stacked(parts_here, [gate_grad])
    other = swap(mine, "core", 1)
    (squares,) = call(
        squares_kernel, "squares", [out_grad, activations, hidden, gate_grad], parts_here[1:], [small], HEAVY, 10
    )
    (squares,) = call(copy_kernel, "held", [squares], [other], [small], SMALL, 1)
    total = squares + swap(squares, "core", 1)
    total = total + swap(total, "z", 1)
    (factor,) = call(
        functools.partial(factor_kernel, math.sqrt(float(model_width * full_hidden * SEQ))),
        "factor",
        [total, swap(total, "z", 2), clip_bounds],
        [*near_hidden, *near_gate],
        [small],
        SMALL,
        1,
        in_specs=[VMEM] * 2 + [SMEM],
    )
    mine_factors, hidden, gate_grad = call(
        pack_kernel,
        "pack",
        [*(shift(factor, "spread", s) for s in STEPS[1:]), hidden, gate_grad],
        [],
        [
            jax.ShapeDtypeStruct((RING - 1, *small.shape), jnp.float32),
            *(jax.ShapeDtypeStruct(v.shape, v.dtype) for v in (hidden, gate_grad)),
        ],
        SMALL,
        1,
        (),
        {RING - 1: 1, RING: 2},
        [VMEM] * (RING - 1) + [ANY] * 2,
        [VMEM] + [ANY] * 2,
    )
    hidden_blocks = [hidden, *near_hidden, shift(hidden, "x", 2)]
    gate_blocks = [gate_grad, *near_gate, shift(gate_grad, "y", 2)]
    factors = [factor, mine_factors, swap(mine_factors, "core", 1)]
    gate_lefts = lefts_of(1, "x", mine, other, factors)
    down_lefts = lefts_of(0, "y", mine, other, factors)
    down = ring_reduce(down_lefts, wide(hidden_blocks, []), "y")
    gated = ring_reduce(gate_lefts, wide(gate_blocks, []), "x")
    return ((down / example_total).astype(jnp.bfloat16), (gated / example_total).astype(jnp.bfloat16))


def solution(mesh):
    torus = Mesh(mesh.devices.reshape(RING, RING, RING, 2), ("x", "y", "z", "core"))
    dp, tensor = ("x", "y"), ("z", "core")
    in_specs = (P(dp, None), P(dp, None), P(dp, tensor), P(dp, tensor), P(None, tensor), P())
    out_specs = (P(dp, tensor), P(dp, tensor))
    return jax.shard_map(local, mesh=torus, in_specs=in_specs, out_specs=out_specs, check_vma=False)
```

```python
import functools
import math

import jax
import jax.numpy as jnp
from jax import lax
from jax.experimental import pallas as pl
from jax.experimental.pallas import tpu as pltpu
from jax.sharding import Mesh, PartitionSpec as P

SEQ = 256
RING = 4
CORES = 2
STEPS = (0, 1, -1, 2)
LANES = 128
MIB = 1024 * 1024
HEAVY = pl.CostEstimate(flops=10**12, bytes_accessed=10**9, transcendentals=0)
SMALL = pl.CostEstimate(flops=0, bytes_accessed=0, transcendentals=0)


def move(value, axes, goal):
    pairs = []
    for x in range(RING):
        for y in range(RING):
            for core in range(2):
                to_x, to_y = goal(x, y, core)
                pairs.append(((x * RING + y) * 2 + core, (to_x % RING * RING + to_y % RING) * 2 + core))
    return lax.ppermute(value, axes, pairs)


def shift(value, axis, step):
    if axis != "spread":
        return lax.ppermute(value, axis, [(i, (i + step) % RING) for i in range(RING)])
    pairs = []
    for x in range(RING):
        for y in range(RING):
            for core in range(2):
                to_x, to_y = ((x + step) % RING, y) if core == 0 else (x, (y + step) % RING)
                pairs.append(((x * RING + y) * 2 + core, (to_x * RING + to_y) * 2 + core))
    return lax.ppermute(value, ("x", "y", "core"), pairs)


def swap(value, axis, bit):
    return lax.ppermute(value, axis, [(i, i ^ bit) for i in range(2 if axis == "core" else RING)])


def dot_last(left, right):
    return lax.dot_general(left, right, (((1,), (1,)), ((), ())), preferred_element_type=jnp.float32)


def dot_first(left, right):
    return lax.dot_general(left, right, (((0,), (0,)), ((), ())), preferred_element_type=jnp.float32)


def around(value, axis):
    return [value] + [shift(value, axis, s) for s in STEPS[1:]]


def ring_reduce(lefts, right, axis):
    up, down, near, own = (dot_last(left, right).astype(jnp.bfloat16) for left in lefts)
    half = own.shape[0] // 2
    wide = lambda v: v.astype(jnp.float32)
    up = shift(up, axis, 1)
    down = shift(down, axis, -1)
    sum_up = shift((wide(near[:half]) + wide(up[:half])).astype(jnp.bfloat16), axis, 1)
    sum_down = shift((wide(near[half:]) + wide(down[:half])).astype(jnp.bfloat16), axis, -1)
    top = wide(own[:half]) + wide(down[half:]) + wide(sum_up)
    bottom = wide(own[half:]) + wide(up[half:]) + wide(sum_down)
    return jnp.concatenate([top, bottom], axis=0)


ANY = pl.BlockSpec(memory_space=pl.ANY)
SMEM = pl.BlockSpec(memory_space=pltpu.SMEM)
VMEM = pl.BlockSpec(memory_space=pltpu.VMEM)


def call(kernel, name, inputs, after, outs, cost, limit, scratch=(), aliases=None, in_specs=None, out_specs=None):
    count = len(inputs)

    def body(*refs):
        kernel(*refs[:count], *refs[count + len(after) :])

    return pl.pallas_call(
        body,
        in_specs=(in_specs or [VMEM] * count) + [ANY] * len(after),
        out_specs=out_specs or [VMEM] * len(outs),
        out_shape=outs,
        scratch_shapes=list(scratch),
        input_output_aliases=aliases or {},
        compiler_params=pltpu.CompilerParams(vmem_limit_bytes=limit * MIB),
        cost_estimate=cost,
        name=name,
    )(*inputs, *after)


def gate_kernel(weight_ref, out_ref, gate_ref, up_ref, *rest):
    hidden_ref, grad_ref = rest[-2:]
    gate = gate_ref[...].astype(jnp.float32)
    up = up_ref[...].astype(jnp.float32)
    sigma = 1.0 / (1.0 + jnp.exp(-gate))
    hidden_ref[...] = (gate * sigma * up).astype(hidden_ref.dtype)
    hidden_grad = dot_last(weight_ref[...], out_ref[...])
    grad_ref[...] = (hidden_grad * up * (sigma * (1.0 + gate * (1.0 - sigma)))).astype(grad_ref.dtype)


def hidden_and_gradient(weight, out_grad, gate, up, after, rows):
    width, depth = weight.shape
    tokens = out_grad.shape[0]
    block = pl.BlockSpec((rows, tokens), lambda i: (i, 0))
    shape = jax.ShapeDtypeStruct((width, tokens), jnp.bfloat16)
    return pl.pallas_call(
        gate_kernel,
        grid=(width // rows,),
        in_specs=[
            pl.BlockSpec((rows, depth), lambda i: (i, 0)),
            pl.BlockSpec((tokens, depth), lambda i: (0, 0)),
            block,
            block,
        ]
        + [ANY] * len(after),
        out_specs=[block, block],
        out_shape=[shape, shape],
        compiler_params=pltpu.CompilerParams(vmem_limit_bytes=50 * MIB),
        cost_estimate=HEAVY,
        name="hidden_and_gradient",
    )(weight, out_grad, gate, up, *after)


def squares_kernel(out_ref, act_ref, hidden_ref, gate_ref, total_ref):
    down = jnp.sum(dot_first(hidden_ref[...], hidden_ref[...]) * dot_last(out_ref[...], out_ref[...]))
    gate = jnp.sum(dot_first(gate_ref[...], gate_ref[...]) * dot_last(act_ref[...], act_ref[...]))
    row = lax.broadcasted_iota(jnp.int32, total_ref.shape, 0)
    total_ref[...] = jnp.where(row < RING, down, gate)


def copy_kernel(source_ref, target_ref):
    target_ref[...] = source_ref[...]


def pack_kernel(*refs):
    for at in range(RING - 1):
        refs[RING + 1][at] = refs[at][...]


def factor_kernel(unit, *refs):
    total = refs[0][...] + refs[1][...]
    row = lax.broadcasted_iota(jnp.int32, total.shape, 0)
    radius = jnp.where(row < RING, refs[2][0], refs[2][1]) * unit
    refs[3][...] = radius / jnp.maximum(jnp.sqrt(total), radius)


def wide_kernel(*refs):
    start = 0
    for block in refs[:-1]:
        refs[-1][:, pl.ds(start, block.shape[1])] = block[...]
        start += block.shape[1]


def wide(blocks):
    width = sum(b.shape[1] for b in blocks)
    shape = jax.ShapeDtypeStruct((blocks[0].shape[0], width), blocks[0].dtype)
    return call(wide_kernel, "wide", blocks, [], [shape], SMALL, 12)[0]


def stack_kernel(*refs):
    blocks, wide_ref = refs[:RING], refs[-1]
    for at, block in enumerate(blocks):
        wide_ref[at] = block[...]


def stacked(blocks, after):
    rows, tokens = blocks[0].shape
    steps = 4
    return pl.pallas_call(
        stack_kernel,
        grid=(steps,),
        in_specs=[pl.BlockSpec((rows // steps, tokens), lambda i: (i, 0))] * RING + [ANY] * len(after),
        out_specs=pl.BlockSpec((RING, rows // steps, tokens), lambda i: (0, i, 0)),
        out_shape=jax.ShapeDtypeStruct((RING, rows, tokens), blocks[0].dtype),
        compiler_params=pltpu.CompilerParams(vmem_limit_bytes=6 * MIB),
        cost_estimate=SMALL,
        name="stack",
    )(*blocks, *after)


def lefts_kernel(owner, axis, mine_ref, other_ref, *refs):
    factor_ref, mine_factors, other_factors = refs[:3]
    outs, held_ref, sems = refs[3 : 3 + RING], refs[-2], refs[-1]
    rows, tokens = outs[0].shape[0], mine_ref.shape[2]
    half = rows // 2
    core, at_axis = lax.axis_index("core"), lax.axis_index(axis)
    far, after, before, own = 2, 1, RING - 1, 0
    halves = ((far, 0), (after, 1), (far, 1), (before, 0), (after, 0), (before, 1), (own, 0), (own, 1))
    waits = []
    for source, here in ((mine_ref, core == owner), (other_ref, core != owner)):
        copies = []
        for at, (goal, part) in enumerate(halves):
            start = pl.multiple_of(lax.rem(at_axis + goal, RING) * rows + part * half, 16)
            for block in range(RING):
                lanes = pl.ds(block * tokens, tokens)
                target = held_ref.at[at // 2, pl.ds(at % 2 * half, half), lanes]
                copies.append(pltpu.make_async_copy(source.at[block, pl.ds(start, half), :], target, sems.at[at, block]))

        @pl.when(here)
        def _():
            for copy in copies:
                copy.start()

        waits = copies
    line = pl.ds(owner * RING, 1)
    scales = [factor_ref[line, :]]
    for at in range(RING - 1):
        scales.append(jnp.where(core == owner, mine_factors[at, line, :], other_factors[at, line, :]))
    scale = jnp.concatenate([f for f in scales for _ in range(tokens // LANES)], axis=1)
    for at, out in enumerate(outs):
        for copy in waits[at * 2 * RING : (at + 1) * 2 * RING]:
            copy.wait()
        out[...] = (held_ref[at].astype(jnp.float32) * scale).astype(out.dtype)


def lefts_of(owner, axis, mine, other, factors, after):
    blocks, depth, tokens = mine.shape
    shape = (depth // RING, blocks * tokens)
    return call(
        functools.partial(lefts_kernel, owner, axis),
        "lefts",
        [mine, other, *factors],
        after,
        [jax.ShapeDtypeStruct(shape, mine.dtype)] * RING,
        SMALL,
        10,
        [pltpu.VMEM((RING, *shape), mine.dtype), pltpu.SemaphoreType.DMA((2 * RING, RING))],
        None,
        [ANY, ANY] + [VMEM] * 3,
    )


def parts_kernel(out_ref, act_ref, *refs):
    targets, window_ref, sems = refs[:RING], refs[RING], refs[RING + 1]
    rows, tokens = targets[0].shape
    owned = rows // RING
    core = lax.axis_index("core")
    at_place = jnp.where(core == 0, lax.axis_index("x"), lax.axis_index("y"))
    places = [lax.rem(at_place + s + RING, RING) for s in STEPS]
    for at in range(RING):
        place = places[at]

        @pl.when(core == 0)
        def _():
            lanes = pl.ds(pl.multiple_of(place * rows, LANES), rows)
            pltpu.make_async_copy(out_ref.at[:, lanes], window_ref.at[at], sems.at[at]).start()

        @pl.when(core != 0)
        def _():
            lanes = pl.ds(at * rows, rows)
            pltpu.make_async_copy(act_ref.at[:, lanes], window_ref.at[at], sems.at[at]).start()

    for at in range(RING):
        pltpu.make_async_copy(out_ref.at[:, pl.ds(0, rows)], window_ref.at[at], sems.at[at]).wait()
    for at in range(RING):
        turned = window_ref[at].T

        @pl.when(core == 0)
        def _():
            targets[at][...] = turned

        @pl.when(core != 0)
        def _():
            for goal in range(RING):
                for place in range(RING):

                    @pl.when(places[goal] == place)
                    def _():
                        targets[goal][pl.ds(at * owned, owned), :] = turned[place * owned : (place + 1) * owned]


def column_parts(out_grad, activations):
    tokens, depth = out_grad.shape
    rows = depth // RING
    return call(
        parts_kernel,
        "column_parts",
        [out_grad, activations],
        [],
        [jax.ShapeDtypeStruct((rows, tokens), out_grad.dtype)] * RING,
        SMALL,
        16,
        [pltpu.VMEM((RING, tokens, rows), out_grad.dtype), pltpu.SemaphoreType.DMA((RING,))],
        None,
        [ANY, ANY],
    )


def local(activations, out_grad, gate_pre, up_pre, down_weight, clip_bounds):
    tokens, model_width = activations.shape
    full_hidden = gate_pre.shape[1] * RING * CORES
    example_total = RING * RING

    parts = column_parts(out_grad, activations)
    parts_here = [parts[0], *(shift(p, "spread", s) for p, s in zip(parts[1:], STEPS[1:], strict=True))]
    hidden, gate_grad = hidden_and_gradient(down_weight.T, out_grad, gate_pre.T, up_pre.T, [parts[0]], 864)
    near_hidden = [shift(hidden, "x", s) for s in STEPS[1:3]]
    near_gate = [shift(gate_grad, "y", s) for s in STEPS[1:3]]

    small = jax.ShapeDtypeStruct((2 * RING, LANES), jnp.float32)
    mine = stacked(parts_here, [gate_grad])
    other = swap(mine, "core", 1)
    (squares,) = call(
        squares_kernel, "squares", [out_grad, activations, hidden, gate_grad], parts_here[1:], [small], HEAVY, 10
    )
    (squares,) = call(copy_kernel, "held", [squares], [other], [small], SMALL, 1)
    total = squares + swap(squares, "core", 1)
    total = total + swap(total, "z", 1)
    (factor,) = call(
        functools.partial(factor_kernel, math.sqrt(float(model_width * full_hidden * SEQ))),
        "factor",
        [total, swap(total, "z", 2), clip_bounds],
        [*near_hidden, *near_gate],
        [small],
        SMALL,
        1,
        in_specs=[VMEM] * 2 + [SMEM],
    )
    mine_factors, hidden, gate_grad = call(
        pack_kernel,
        "pack",
        [*(shift(factor, "spread", s) for s in STEPS[1:]), hidden, gate_grad],
        [],
        [
            jax.ShapeDtypeStruct((RING - 1, *small.shape), jnp.float32),
            *(jax.ShapeDtypeStruct(v.shape, v.dtype) for v in (hidden, gate_grad)),
        ],
        SMALL,
        1,
        (),
        {RING - 1: 1, RING: 2},
        [VMEM] * (RING - 1) + [ANY] * 2,
        [VMEM] + [ANY] * 2,
    )
    far_hidden, far_gate = shift(hidden, "x", 2), shift(gate_grad, "y", 2)
    near_hidden, near_gate = wide([hidden, *near_hidden]), wide([gate_grad, *near_gate])
    factors = [factor, mine_factors, swap(mine_factors, "core", 1)]
    gate_lefts = lefts_of(1, "x", mine, other, factors, [near_hidden, near_gate])
    down_lefts = lefts_of(0, "y", mine, other, factors, [gate_lefts[0]])
    down = ring_reduce(down_lefts, wide([near_hidden, far_hidden]), "y")
    gated = ring_reduce(gate_lefts, wide([near_gate, far_gate]), "x")
    return ((down / example_total).astype(jnp.bfloat16), (gated / example_total).astype(jnp.bfloat16))


def solution(mesh):
    torus = Mesh(mesh.devices.reshape(RING, RING, RING, 2), ("x", "y", "z", "core"))
    dp, tensor = ("x", "y"), ("z", "core")
    in_specs = (P(dp, None), P(dp, None), P(dp, tensor), P(dp, tensor), P(None, tensor), P())
    out_specs = (P(dp, tensor), P(dp, tensor))
    return jax.shard_map(local, mesh=torus, in_specs=in_specs, out_specs=out_specs, check_vma=False)
```

```python
import functools
import math

import jax
import jax.numpy as jnp
from jax import lax
from jax.experimental import pallas as pl
from jax.experimental.pallas import tpu as pltpu
from jax.sharding import Mesh, PartitionSpec as P

SEQ = 256
RING = 4
CORES = 2
STEPS = (0, 1, -1, 2)
LANES = 128
MIB = 1024 * 1024
HEAVY = pl.CostEstimate(flops=10**12, bytes_accessed=10**9, transcendentals=0)
SMALL = pl.CostEstimate(flops=0, bytes_accessed=0, transcendentals=0)


def move(value, axes, goal):
    pairs = []
    for x in range(RING):
        for y in range(RING):
            for core in range(2):
                to_x, to_y = goal(x, y, core)
                pairs.append(((x * RING + y) * 2 + core, (to_x % RING * RING + to_y % RING) * 2 + core))
    return lax.ppermute(value, axes, pairs)


def shift(value, axis, step):
    if axis != "spread":
        return lax.ppermute(value, axis, [(i, (i + step) % RING) for i in range(RING)])
    pairs = []
    for x in range(RING):
        for y in range(RING):
            for core in range(2):
                to_x, to_y = ((x + step) % RING, y) if core == 0 else (x, (y + step) % RING)
                pairs.append(((x * RING + y) * 2 + core, (to_x * RING + to_y) * 2 + core))
    return lax.ppermute(value, ("x", "y", "core"), pairs)


def swap(value, axis, bit):
    return lax.ppermute(value, axis, [(i, i ^ bit) for i in range(2 if axis == "core" else RING)])


def dot_last(left, right):
    return lax.dot_general(left, right, (((1,), (1,)), ((), ())), preferred_element_type=jnp.float32)


def dot_first(left, right):
    return lax.dot_general(left, right, (((0,), (0,)), ((), ())), preferred_element_type=jnp.float32)


def around(value, axis):
    return [value] + [shift(value, axis, s) for s in STEPS[1:]]


def ring_reduce(lefts, right, axis):
    up, down, near, own = (dot_last(left, right).astype(jnp.bfloat16) for left in lefts)
    half = own.shape[0] // 2
    wide = lambda v: v.astype(jnp.float32)
    up = shift(up, axis, 1)
    down = shift(down, axis, -1)
    sum_up = shift((wide(near[:half]) + wide(up[:half])).astype(jnp.bfloat16), axis, 1)
    sum_down = shift((wide(near[half:]) + wide(down[:half])).astype(jnp.bfloat16), axis, -1)
    top = wide(own[:half]) + wide(down[half:]) + wide(sum_up)
    bottom = wide(own[half:]) + wide(up[half:]) + wide(sum_down)
    return jnp.concatenate([top, bottom], axis=0)


ANY = pl.BlockSpec(memory_space=pl.ANY)
SMEM = pl.BlockSpec(memory_space=pltpu.SMEM)
VMEM = pl.BlockSpec(memory_space=pltpu.VMEM)


def call(kernel, name, inputs, after, outs, cost, limit, scratch=(), aliases=None, in_specs=None, out_specs=None):
    count = len(inputs)

    def body(*refs):
        kernel(*refs[:count], *refs[count + len(after) :])

    return pl.pallas_call(
        body,
        in_specs=(in_specs or [VMEM] * count) + [ANY] * len(after),
        out_specs=out_specs or [VMEM] * len(outs),
        out_shape=outs,
        scratch_shapes=list(scratch),
        input_output_aliases=aliases or {},
        compiler_params=pltpu.CompilerParams(vmem_limit_bytes=limit * MIB),
        cost_estimate=cost,
        name=name,
    )(*inputs, *after)


def gate_kernel(weight_ref, out_ref, gate_ref, up_ref, *rest):
    hidden_ref, grad_ref = rest[-2:]
    gate = gate_ref[...].astype(jnp.float32)
    up = up_ref[...].astype(jnp.float32)
    sigma = 1.0 / (1.0 + jnp.exp(-gate))
    hidden_ref[...] = (gate * sigma * up).astype(hidden_ref.dtype)
    hidden_grad = dot_last(weight_ref[...], out_ref[...])
    grad_ref[...] = (hidden_grad * up * (sigma * (1.0 + gate * (1.0 - sigma)))).astype(grad_ref.dtype)


def hidden_and_gradient(weight, out_grad, gate, up, after, rows):
    width, depth = weight.shape
    tokens = out_grad.shape[0]
    block = pl.BlockSpec((rows, tokens), lambda i: (i, 0))
    shape = jax.ShapeDtypeStruct((width, tokens), jnp.bfloat16)
    return pl.pallas_call(
        gate_kernel,
        grid=(width // rows,),
        in_specs=[
            pl.BlockSpec((rows, depth), lambda i: (i, 0)),
            pl.BlockSpec((tokens, depth), lambda i: (0, 0)),
            block,
            block,
        ]
        + [ANY] * len(after),
        out_specs=[block, block],
        out_shape=[shape, shape],
        compiler_params=pltpu.CompilerParams(vmem_limit_bytes=50 * MIB),
        cost_estimate=HEAVY,
        name="hidden_and_gradient",
    )(weight, out_grad, gate, up, *after)


def squares_kernel(out_ref, act_ref, hidden_ref, gate_ref, total_ref):
    down = jnp.sum(dot_first(hidden_ref[...], hidden_ref[...]) * dot_last(out_ref[...], out_ref[...]))
    gate = jnp.sum(dot_first(gate_ref[...], gate_ref[...]) * dot_last(act_ref[...], act_ref[...]))
    row = lax.broadcasted_iota(jnp.int32, total_ref.shape, 0)
    total_ref[...] = jnp.where(row < RING, down, gate)


def copy_kernel(source_ref, target_ref):
    target_ref[...] = source_ref[...]


def pack_kernel(*refs):
    for at in range(RING - 1):
        refs[RING - 1][at] = refs[at][...]


def held_kernel(*refs):
    pass


def held_back(values, after):
    count = len(values)
    shapes = [jax.ShapeDtypeStruct(v.shape, v.dtype) for v in values]
    aliases = {at: at for at in range(count)}
    return call(held_kernel, "held_back", values, after, shapes, SMALL, 1, (), aliases, [ANY] * count, [ANY] * count)


def factor_kernel(unit, *refs):
    total = refs[0][...] + refs[1][...]
    row = lax.broadcasted_iota(jnp.int32, total.shape, 0)
    radius = jnp.where(row < RING, refs[2][0], refs[2][1]) * unit
    refs[3][...] = radius / jnp.maximum(jnp.sqrt(total), radius)


def wide_kernel(*refs):
    tokens = refs[0].shape[1]
    for at in range(RING):
        refs[RING][:, pl.ds(at * tokens, tokens)] = refs[at][...]


def wide(blocks, after):
    rows, tokens = blocks[0].shape
    shape = jax.ShapeDtypeStruct((rows, RING * tokens), blocks[0].dtype)
    return call(wide_kernel, "wide", blocks, after, [shape], SMALL, 12)[0]


def stack_kernel(*refs):
    blocks, wide_ref = refs[:RING], refs[-1]
    for at, block in enumerate(blocks):
        wide_ref[at] = block[...]


def stacked(blocks, after):
    rows, tokens = blocks[0].shape
    steps = 4
    return pl.pallas_call(
        stack_kernel,
        grid=(steps,),
        in_specs=[pl.BlockSpec((rows // steps, tokens), lambda i: (i, 0))] * RING + [ANY] * len(after),
        out_specs=pl.BlockSpec((RING, rows // steps, tokens), lambda i: (0, i, 0)),
        out_shape=jax.ShapeDtypeStruct((RING, rows, tokens), blocks[0].dtype),
        compiler_params=pltpu.CompilerParams(vmem_limit_bytes=6 * MIB),
        cost_estimate=SMALL,
        name="stack",
    )(*blocks, *after)


def lefts_kernel(owner, axis, mine_ref, other_ref, *refs):
    factor_ref, mine_factors, other_factors = refs[:3]
    outs, held_ref, sems = refs[3 : 3 + RING], refs[-2], refs[-1]
    rows, tokens = outs[0].shape[0], mine_ref.shape[2]
    half = rows // 2
    core, at_axis = lax.axis_index("core"), lax.axis_index(axis)
    far, after, before, own = 2, 1, RING - 1, 0
    halves = ((far, 0), (after, 1), (far, 1), (before, 0), (after, 0), (before, 1), (own, 0), (own, 1))
    waits = []
    for source, here in ((mine_ref, core == owner), (other_ref, core != owner)):
        copies = []
        for at, (goal, part) in enumerate(halves):
            start = pl.multiple_of(lax.rem(at_axis + goal, RING) * rows + part * half, 16)
            for block in range(RING):
                lanes = pl.ds(block * tokens, tokens)
                target = held_ref.at[at // 2, pl.ds(at % 2 * half, half), lanes]
                copies.append(pltpu.make_async_copy(source.at[block, pl.ds(start, half), :], target, sems.at[at, block]))

        @pl.when(here)
        def _():
            for copy in copies:
                copy.start()

        waits = copies
    line = pl.ds(owner * RING, 1)
    scales = [factor_ref[line, :]]
    for at in range(RING - 1):
        scales.append(jnp.where(core == owner, mine_factors[at, line, :], other_factors[at, line, :]))
    scale = jnp.concatenate([f for f in scales for _ in range(tokens // LANES)], axis=1)
    for at, out in enumerate(outs):
        for copy in waits[at * 2 * RING : (at + 1) * 2 * RING]:
            copy.wait()
        out[...] = (held_ref[at].astype(jnp.float32) * scale).astype(out.dtype)


def lefts_of(owner, axis, mine, other, factors):
    blocks, depth, tokens = mine.shape
    shape = (depth // RING, blocks * tokens)
    return call(
        functools.partial(lefts_kernel, owner, axis),
        "lefts",
        [mine, other, *factors],
        [],
        [jax.ShapeDtypeStruct(shape, mine.dtype)] * RING,
        SMALL,
        10,
        [pltpu.VMEM((RING, *shape), mine.dtype), pltpu.SemaphoreType.DMA((2 * RING, RING))],
        None,
        [ANY, ANY] + [VMEM] * 3,
    )


def parts_kernel(out_ref, act_ref, *refs):
    targets, window_ref, sems = refs[:RING], refs[RING], refs[RING + 1]
    rows, tokens = targets[0].shape
    owned = rows // RING
    core = lax.axis_index("core")
    at_place = jnp.where(core == 0, lax.axis_index("x"), lax.axis_index("y"))
    places = [lax.rem(at_place + s + RING, RING) for s in STEPS]
    for at in range(RING):
        place = places[at]

        @pl.when(core == 0)
        def _():
            lanes = pl.ds(pl.multiple_of(place * rows, LANES), rows)
            pltpu.make_async_copy(out_ref.at[:, lanes], window_ref.at[at], sems.at[at]).start()

        @pl.when(core != 0)
        def _():
            lanes = pl.ds(at * rows, rows)
            pltpu.make_async_copy(act_ref.at[:, lanes], window_ref.at[at], sems.at[at]).start()

    for at in range(RING):
        pltpu.make_async_copy(out_ref.at[:, pl.ds(0, rows)], window_ref.at[at], sems.at[at]).wait()
    for at in range(RING):
        turned = window_ref[at].T

        @pl.when(core == 0)
        def _():
            targets[at][...] = turned

        @pl.when(core != 0)
        def _():
            for goal in range(RING):
                for place in range(RING):

                    @pl.when(places[goal] == place)
                    def _():
                        targets[goal][pl.ds(at * owned, owned), :] = turned[place * owned : (place + 1) * owned]


def column_parts(out_grad, activations):
    tokens, depth = out_grad.shape
    rows = depth // RING
    return call(
        parts_kernel,
        "column_parts",
        [out_grad, activations],
        [],
        [jax.ShapeDtypeStruct((rows, tokens), out_grad.dtype)] * RING,
        SMALL,
        16,
        [pltpu.VMEM((RING, tokens, rows), out_grad.dtype), pltpu.SemaphoreType.DMA((RING,))],
        None,
        [ANY, ANY],
    )


def local(activations, out_grad, gate_pre, up_pre, down_weight, clip_bounds):
    tokens, model_width = activations.shape
    full_hidden = gate_pre.shape[1] * RING * CORES
    example_total = RING * RING

    parts = column_parts(out_grad, activations)
    parts_here = [parts[0], *(shift(p, "spread", s) for p, s in zip(parts[1:], STEPS[1:], strict=True))]
    hidden, gate_grad = hidden_and_gradient(down_weight.T, out_grad, gate_pre.T, up_pre.T, [parts[0]], 864)
    near_hidden = [shift(hidden, "x", s) for s in STEPS[1:3]]
    near_gate = [shift(gate_grad, "y", s) for s in STEPS[1:3]]

    small = jax.ShapeDtypeStruct((2 * RING, LANES), jnp.float32)
    mine = stacked(parts_here, [gate_grad])
    other = swap(mine, "core", 1)
    (squares,) = call(
        squares_kernel, "squares", [out_grad, activations, hidden, gate_grad], parts_here[1:], [small], HEAVY, 10
    )
    (squares,) = call(copy_kernel, "held", [squares], [other], [small], SMALL, 1)
    total = squares + swap(squares, "core", 1)
    total = total + swap(total, "z", 1)
    (factor,) = call(
        functools.partial(factor_kernel, math.sqrt(float(model_width * full_hidden * SEQ))),
        "factor",
        [total, swap(total, "z", 2), clip_bounds],
        [*near_hidden, *near_gate],
        [small],
        SMALL,
        1,
        in_specs=[VMEM] * 2 + [SMEM],
    )
    given = [shift(factor, "spread", s) for s in STEPS[1:]]
    hidden, gate_grad = held_back([hidden, gate_grad], given[:2])
    (mine_factors,) = call(
        pack_kernel, "pack", given, [], [jax.ShapeDtypeStruct((RING - 1, *small.shape), jnp.float32)], SMALL, 1
    )
    hidden_blocks = [hidden, *near_hidden, shift(hidden, "x", 2)]
    gate_blocks = [gate_grad, *near_gate, shift(gate_grad, "y", 2)]
    factors = [factor, mine_factors, swap(mine_factors, "core", 1)]
    gate_lefts = lefts_of(1, "x", mine, other, factors)
    down_lefts = lefts_of(0, "y", mine, other, factors)
    down = ring_reduce(down_lefts, wide(hidden_blocks, []), "y")
    gated = ring_reduce(gate_lefts, wide(gate_blocks, []), "x")
    return ((down / example_total).astype(jnp.bfloat16), (gated / example_total).astype(jnp.bfloat16))


def solution(mesh):
    torus = Mesh(mesh.devices.reshape(RING, RING, RING, 2), ("x", "y", "z", "core"))
    dp, tensor = ("x", "y"), ("z", "core")
    in_specs = (P(dp, None), P(dp, None), P(dp, tensor), P(dp, tensor), P(None, tensor), P())
    out_specs = (P(dp, tensor), P(dp, tensor))
    return jax.shard_map(local, mesh=torus, in_specs=in_specs, out_specs=out_specs, check_vma=False)
```
